256 devices in a mesh: dp: 32 (over z, x_lo, core), rep: 8 (over x_hi, y).
Axes of the slice: x: 4 (x_hi: 2, x_lo: 2; x = x_hi * 2 + x_lo), y: 4, z: 8, core: 2. Of those that a mesh axis runs over, the one named last changes fastest.
Arguments:
- image_emb: bfloat16 [32768, 512], P(('rep', 'dp')), parts along dimension 0, may hold values from -48 to 48
- text_emb: bfloat16 [32768, 512], P(('rep', 'dp')), parts along dimension 0, may hold values from -3 to 3
- labels: int32 [32768], P(('rep', 'dp')), parts along dimension 0, may hold values from 0 to 4095, as said below
Outputs:
- image_grad: float32 [32768, 512], P(('rep', 'dp')), parts along dimension 0
- text_grad: float32 [32768, 512], P(('rep', 'dp')), parts along dimension 0
The draws below stay inside these ranges and needn't reach their ends.
There are 8 independent parts, one for each index of `rep`. The reference program is written for one: setup_inputs(seed, part) draws one part's arguments, and reference() takes and returns one part's arrays. A program takes and returns all parts, laid end to end along the dimension named above; each array names one. Nothing has to cross between parts.
Inputs may be any that keep to these rules, and one draw needn't show every extreme that they name: `labels`: each image row's positive text row lies in the same aligned block of 128 rows, and every text row is the positive of exactly one image row.
All inputs are finite; a program needn't handle non-finite values.
Results may differ from the reference program's by a relative error of at most 0.0017.
Values may be sent and summed in bfloat16 or wider, within the bound.
A program may use at most 64 MiB of HBM per device.

```python
import math
import jax
import jax.numpy as jnp
from jax import lax

D = 512
ROWS = 128
TOKENS = 4096


def embed_pair(key, strength_on):
    subkeys = jax.random.split(key, 6)
    block_count = TOKENS // ROWS
    row_ids = jnp.arange(TOKENS, dtype=jnp.int32)
    text_emb = jnp.clip(jax.random.normal(subkeys[0], (TOKENS, D), jnp.float32), -4.0, 4.0) * D ** (-0.5)
    text_scale = jnp.exp(jax.random.uniform(subkeys[1], (TOKENS,), jnp.float32, math.log(0.5), math.log(5.0)))
    text_emb = text_emb * text_scale[:, None]
    ramp = 1.0 + 2.0 * (row_ids // ROWS).astype(jnp.float32) / max(block_count - 1, 1)
    image_scale = jnp.exp(jax.random.uniform(subkeys[2], (TOKENS,), jnp.float32, math.log(0.25), math.log(1.0))) * ramp
    image_emb = jnp.clip(jax.random.normal(subkeys[3], (TOKENS, D), jnp.float32), -4.0, 4.0) * D ** (-0.5)
    image_emb = image_emb * image_scale[:, None]
    pair_on = (jax.random.uniform(subkeys[4], (TOKENS // 2,), jnp.float32) < 0.125).astype(jnp.float32) * strength_on
    odd_rows = (row_ids % 2).astype(jnp.float32)
    duplicate = pair_on[row_ids // 2] * odd_rows
    text_emb = text_emb * (1.0 - duplicate)[:, None]
    partner = 2 * ((row_ids // 2 + TOKENS // 4) % (TOKENS // 2))
    image_on = pair_on[partner // 2] * (jax.random.uniform(subkeys[5], (TOKENS,), jnp.float32) < 0.5).astype(jnp.float32)
    image_emb = image_emb * (1.0 - image_on)[:, None]
    return (image_emb, text_emb)


def draw_image_emb(key, part):
    image_emb, text_emb = embed_pair(key, 0.0)
    return image_emb.astype(jnp.bfloat16)


def draw_text_emb(key, part):
    image_emb, text_emb = embed_pair(key, 0.0)
    return text_emb.astype(jnp.bfloat16)


def shuffle_block(block_key):
    return jax.random.permutation(block_key, ROWS)


def draw_labels(key, part):
    key = jax.random.fold_in(key, 7)
    block_count = TOKENS // ROWS
    subkeys = jax.random.split(key, block_count)
    shuffles = jax.vmap(shuffle_block)(subkeys).astype(jnp.int32)
    offsets = ROWS * jnp.arange(block_count, dtype=jnp.int32)
    return (shuffles + offsets[:, None]).reshape(TOKENS).astype(jnp.int32)


def setup_inputs(seed: int = 0, part: int = 0) -> dict:
    arg_keys = jax.random.split(jax.random.key(seed), 4)
    own_keys = jax.random.split(jax.random.fold_in(arg_keys[3], part), 4)
    image_emb = draw_image_emb(jax.random.fold_in(jax.random.fold_in(arg_keys[3], part), 71), part)
    text_emb = draw_text_emb(jax.random.fold_in(jax.random.fold_in(arg_keys[3], part), 71), part)
    labels = draw_labels(jax.random.fold_in(jax.random.fold_in(arg_keys[3], part), 71), part)
    return {"image_emb": image_emb, "text_emb": text_emb, "labels": labels}


logit_scale = 10.0


def block_scores(image_rows, text_emb):
    return logit_scale * jnp.dot(image_rows, text_emb.T, preferred_element_type=jnp.float32)


def reference(image_emb, text_emb, labels):
    block_count = TOKENS // ROWS
    image_blocks = image_emb.reshape(block_count, ROWS, D)
    label_blocks = labels.reshape(block_count, ROWS)
    column_ids = jnp.arange(TOKENS, dtype=jnp.int32)

    def first_pass(running, image_rows):
        col_peak, col_mass = running
        scores = block_scores(image_rows, text_emb)
        row_peak = jnp.max(scores, axis=1)
        row_lse = row_peak + jnp.log(jnp.sum(jnp.exp(scores - row_peak[:, None]), axis=1))
        new_peak = jnp.maximum(col_peak, jnp.max(scores, axis=0))
        col_mass = col_mass * jnp.exp(col_peak - new_peak) + jnp.sum(jnp.exp(scores - new_peak[None, :]), axis=0)
        return (new_peak, col_mass), row_lse

    start_state = (jnp.full((TOKENS,), -jnp.inf, jnp.float32), jnp.zeros((TOKENS,), jnp.float32))
    (col_peak, col_mass), row_lse = lax.scan(first_pass, start_state, image_blocks)
    col_lse = col_peak + jnp.log(col_mass)

    def second_pass(text_total, inputs):
        image_rows, label_rows, lse_rows = inputs
        scores = block_scores(image_rows, text_emb)
        positive = (column_ids[None, :] == label_rows[:, None]).astype(jnp.float32)
        weights = (0.5 * jnp.exp(scores - lse_rows[:, None]) + 0.5 * jnp.exp(scores - col_lse[None, :]) - positive).astype(jnp.bfloat16)
        image_part = logit_scale * jnp.dot(weights, text_emb, preferred_element_type=jnp.float32)
        text_part = logit_scale * jnp.dot(weights.T, image_rows, preferred_element_type=jnp.float32)
        return text_total + text_part, image_part

    text_grad, image_parts = lax.scan(second_pass, jnp.zeros((TOKENS, D), jnp.float32), (image_blocks, label_blocks, row_lse))
    return image_parts.reshape(TOKENS, D), text_grad
```

```python
import functools
import math

import jax
import jax.numpy as jnp
from jax import lax
from jax.experimental import pallas as pl
from jax.experimental.pallas import tpu as pltpu
from jax.sharding import PartitionSpec as P

logit_scale = 10.0
log2_scale = logit_scale / math.log(2.0)

ROWS = 128
HALF = 64
CHUNK = 32
NCH = ROWS // CHUNK
PLANES = 8
MESH = pl.DeviceIdType.MESH

OFFSETS = (0, -1, -2, -3, 1, 2, 3, 4)
SLOT_OF = {o: i for i, o in enumerate(OFFSETS)}
SLOT_OF[-4] = 7


def scores_of(rows, cols):
    return log2_scale * lax.dot_general(
        rows, cols, (((1,), (1,)), ((), ())), preferred_element_type=jnp.float32
    )


def to_lanes(column):
    return jnp.transpose(jnp.broadcast_to(column, (ROWS, ROWS)))[0:1, :]


def to_sublanes(lanes):
    return jnp.transpose(jnp.broadcast_to(lanes, (ROWS, ROWS)))


def log_add(a, b):
    top = jnp.maximum(a, b)
    return top + jnp.log2(jnp.exp2(a - top) + jnp.exp2(b - top))


def kernel(
    img_ref, txt_ref, lab_ref, oimg_ref, otxt_ref,
    cimg, ctxt, rimg, rtxt, scores, gimg, gtxt, gsend, grecv,
    colp, sibrx, chipcol, zrx, colf, colx, rowp, rowrx, rowabs, rsub, csub,
    ring_s, ring_r, sib_s, sib_r, z_s, z_r, misc_s, misc_r, loc_s,
):
    me = lax.axis_index("dp")
    z, x, k = me // 4, (me // 2) % 2, me % 2

    def device(plane, column, core):
        return {"dp": lax.rem(plane + PLANES, PLANES) * 4 + column * 2 + core}

    right, left = device(z + 1, x, k), device(z - 1, x, k)
    nbr, sib = device(z, 1 - x, k), device(z, x, 1 - k)
    held = (ctxt, cimg)
    rows_of = (rtxt, rimg)
    given = (txt_ref, img_ref)

    def remote(src, dst, send, recv, to):
        return pltpu.make_async_remote_copy(
            src_ref=src, dst_ref=dst, send_sem=send, recv_sem=recv, device_id=to, device_id_type=MESH
        )

    def plane_of(slot):
        off = OFFSETS[slot] if isinstance(slot, int) else jnp.where(slot < 4, -slot, slot - 3)
        return lax.rem(z + off + PLANES, PLANES)

    def slot(d, s):
        return 0 if s == 0 else 7 if s == 4 else s + 3 * d

    def valid(d, s, c):
        return s < 4 or (c < NCH // 2) == (d == 0)

    def ring(a, d, s, c):
        part = pl.ds(c * CHUNK, CHUNK)
        i = ((a * 2 + d) * 4 + s - 1) * NCH + c
        src = given[a].at[part] if s == 1 else held[a].at[slot(d, s - 1), 0, part]
        return remote(src, held[a].at[slot(d, s), 0, part], ring_s.at[i], ring_r.at[i], (right, left)[d])

    def to_sib(a, d, s):
        i = (a * 2 + d) * 5 + s
        if s == 0:
            src, dst = given[a], held[a].at[0, 1]
        elif s == 4:
            part = pl.ds(HALF * d, HALF)
            src, dst = held[a].at[7, 0, part], held[a].at[7, 1, part]
        else:
            src, dst = held[a].at[slot(d, s), 0], held[a].at[slot(d, s), 1]
        return remote(src, dst, sib_s.at[i], sib_r.at[i], sib)

    def misc(i, src, dst, to):
        return remote(src, dst, misc_s.at[i], misc_r.at[i], to)

    def rows_to_nbr(a):
        return misc(a, given[a], rows_of[a].at[0], nbr)

    def z_col(p):
        return remote(
            chipcol, zrx.at[SLOT_OF[-OFFSETS[p]]], z_s.at[p], z_r.at[SLOT_OF[-OFFSETS[p]]],
            device(z + OFFSETS[p], x, k),
        )

    def z_row(p):
        return remote(
            rowabs.at[0, z], rowabs.at[0, z], z_s.at[8 + p], z_r.at[8 + SLOT_OF[-OFFSETS[p]]],
            device(z + OFFSETS[p], x, k),
        )

    def z_row_arrives(p):
        return remote(rowabs.at[0, plane_of(p)], rowabs.at[0, plane_of(p)], z_s.at[8 + p], z_r.at[8 + p], right)

    def z_col_arrives(p):
        return remote(chipcol, zrx.at[p], z_s.at[p], z_r.at[p], right)

    own = [
        pltpu.make_async_copy(given[0], ctxt.at[0, 0], loc_s.at[0]),
        pltpu.make_async_copy(given[1], rimg.at[1], loc_s.at[1]),
        pltpu.make_async_copy(given[1], cimg.at[0, 0], loc_s.at[2]),
        pltpu.make_async_copy(given[0], rtxt.at[1], loc_s.at[3]),
    ]
    for c in own:
        c.start()
    barrier = pltpu.get_barrier_semaphore()
    peers = [device(z + o, x, k) for o in OFFSETS[1:]] + [nbr, sib]
    for p in peers:
        pl.semaphore_signal(barrier, inc=1, device_id=p, device_id_type=MESH)
    pl.semaphore_wait(barrier, len(peers))

    def first_sends(a):
        for c in range(NCH):
            for d in range(2):
                ring(a, d, 1, c).start()

    def ring_step(a, s):
        for c in range(NCH):
            for d in range(2):
                if valid(d, s, c):
                    ring(a, d, s, c).wait_recv()
                    if s < 4 and valid(d, s + 1, c):
                        ring(a, d, s + 1, c).start()
        for d in range(2):
            to_sib(a, d, s).start()

    def from_sib(a, s):
        for d in range(2):
            to_sib(a, d, s).wait_recv()

    first_sends(0)
    to_sib(0, 0, 0).start()
    rows_to_nbr(1).start()
    first_sends(1)
    to_sib(1, 0, 0).start()
    rows_to_nbr(0).start()

    row_peak = jnp.full((2 * ROWS, 1), -jnp.inf, jnp.float32)
    row_mass = jnp.zeros((2 * ROWS, 1), jnp.float32)

    def image_tile(q, peak, mass):
        s = scores_of(rimg[...].reshape(2 * ROWS, -1), ctxt[q].reshape(2 * ROWS, -1))
        scores[q] = s
        top = jnp.max(s, axis=0, keepdims=True)
        col = top + jnp.log2(jnp.sum(jnp.exp2(s - top), axis=0, keepdims=True))
        for kr in range(2):
            colp[kr, plane_of(q)] = col[:, kr * ROWS : (kr + 1) * ROWS]
        new_peak = jnp.maximum(peak, jnp.max(s, axis=1, keepdims=True))
        mass = mass * jnp.exp2(peak - new_peak) + jnp.sum(jnp.exp2(s - new_peak), axis=1, keepdims=True)
        return new_peak, mass

    ring_step(0, 1)
    own[0].wait()
    own[1].wait()
    rows_to_nbr(1).wait_recv()
    to_sib(0, 0, 0).wait_recv()
    row_peak, row_mass = image_tile(0, row_peak, row_mass)
    ring_step(0, 2)
    from_sib(0, 1)
    for q in (1, 4):
        row_peak, row_mass = image_tile(q, row_peak, row_mass)
    ring_step(0, 3)
    ring_step(1, 1)
    from_sib(0, 2)
    for q in (2, 5):
        row_peak, row_mass = image_tile(q, row_peak, row_mass)
    ring_step(0, 4)
    from_sib(0, 3)
    for q in (3, 6):
        row_peak, row_mass = image_tile(q, row_peak, row_mass)
    from_sib(0, 4)
    row_peak, row_mass = image_tile(7, row_peak, row_mass)

    col_to_sib = misc(2, colp.at[1], sibrx, sib)
    col_to_sib.start()
    row_part = row_peak + jnp.log2(row_mass)
    rowp[0] = to_lanes(row_part[:ROWS])
    rowp[1] = to_lanes(row_part[ROWS:])
    row_to_nbr = misc(3, rowp, rowrx, nbr)
    row_to_nbr.start()
    ring_step(1, 2)
    col_to_sib.wait_recv()
    chipcol[...] = log_add(colp[0], sibrx[...])
    for p in range(1, 8):
        z_col(p).start()
    row_to_nbr.wait_recv()
    row_nbr = log_add(rowp[0], rowrx[1])
    row_own = log_add(rowp[1], rowrx[0])
    rowabs[0, z] = row_own
    for p in range(1, 8):
        z_row(p).start()
    rsub[:ROWS] = to_sublanes(row_nbr + 1.0)
    rsub[ROWS:] = to_sublanes(row_own + 1.0)
    ring_step(1, 3)
    for p in range(1, 8):
        z_col_arrives(p).wait_recv()
    parts = [chipcol[...]] + [zrx[p] for p in range(1, 8)]
    top = functools.reduce(jnp.maximum, parts)
    mass = sum(jnp.exp2(p - top) for p in parts)
    colf[0] = top + jnp.log2(mass)
    colf_to_sib = misc(4, colf.at[0], colf.at[1], sib)
    colf_to_sib.start()
    colf_to_nbr = misc(5, colf.at[0, z], colx.at[0], nbr)
    colf_to_nbr.start()
    colf_to_sib.wait_recv()

    def lanes_of(ref, q):
        plane = plane_of(q)
        return jnp.concatenate([ref[0, plane], ref[1, plane]], axis=1) + 1.0

    def weights_of(s, sub, lanes):
        return jnp.exp2(s - jnp.concatenate([sub, sub], axis=1)) + jnp.exp2(s - lanes)

    def with_positive(w, positive):
        zero = jnp.zeros((ROWS, ROWS), jnp.float32)
        mask = jnp.concatenate([zero, positive.astype(jnp.float32)], axis=0)
        return w - jnp.concatenate([mask, jnp.zeros((2 * ROWS, ROWS), jnp.float32)], axis=1)

    labels = lab_ref[...] - me * ROWS
    label_rows = to_sublanes(labels.astype(jnp.float32))
    lane_ids = lax.broadcasted_iota(jnp.int32, (ROWS, ROWS), 1)
    row_ids = lax.broadcasted_iota(jnp.int32, (ROWS, ROWS), 0)

    def image_weights(q):
        return weights_of(scores[q], rsub[...], lanes_of(colf, q))

    def image_product(q, w):
        return jnp.dot(
            w.astype(jnp.bfloat16), ctxt[q].reshape(2 * ROWS, -1), preferred_element_type=jnp.float32
        )

    gimg[...] = image_product(0, with_positive(image_weights(0), label_rows == lane_ids.astype(jnp.float32)))

    def image_turn(q, carry):
        gimg[...] += image_product(q, image_weights(q))
        return carry

    lax.fori_loop(1, 8, image_turn, 0)
    gsend[0] = (logit_scale * gimg[:ROWS]).astype(jnp.bfloat16)
    gimg_to_nbr = misc(6, gsend.at[0], grecv.at[0], nbr)
    gimg_to_nbr.start()

    for p in range(1, 8):
        z_row_arrives(p).wait_recv()
    rowabs_to_sib = misc(7, rowabs.at[0], rowabs.at[1], sib)
    rowabs_to_sib.start()
    ring_step(1, 4)
    colf_to_nbr.wait_recv()
    csub[:ROWS] = to_sublanes(colx[0] + 1.0)
    csub[ROWS:] = to_sublanes(colf[0, z] + 1.0)
    rowabs_to_sib.wait_recv()
    own[2].wait()
    own[3].wait()
    rows_to_nbr(0).wait_recv()
    to_sib(1, 0, 0).wait_recv()
    from_sib(1, 1)
    from_sib(1, 2)
    from_sib(1, 3)

    def text_weights(q):
        s = scores_of(rtxt[...].reshape(2 * ROWS, -1), cimg[q].reshape(2 * ROWS, -1))
        return weights_of(s, csub[...], lanes_of(rowabs, q))

    def text_product(q, w):
        return jnp.dot(
            w.astype(jnp.bfloat16), cimg[q].reshape(2 * ROWS, -1), preferred_element_type=jnp.float32
        )

    gtxt[...] = text_product(0, with_positive(text_weights(0), labels == row_ids))

    def text_turn(q, carry):
        gtxt[...] += text_product(q, text_weights(q))
        return carry

    lax.fori_loop(1, 7, text_turn, 0)
    from_sib(1, 4)
    text_turn(7, 0)
    gsend[1] = (logit_scale * gtxt[:ROWS]).astype(jnp.bfloat16)
    gtxt_to_nbr = misc(8, gsend.at[1], grecv.at[1], nbr)
    gtxt_to_nbr.start()

    gimg_to_nbr.wait_recv()
    oimg_ref[...] = logit_scale * gimg[ROWS:] + grecv[0].astype(jnp.float32)

    for a in range(2):
        for d in range(2):
            for s in range(1, 5):
                for c in range(NCH):
                    if valid(d, s, c):
                        ring(a, d, s, c).wait_send()
                to_sib(a, d, s).wait_send()
        to_sib(a, 0, 0).wait_send()
        rows_to_nbr(a).wait_send()
    for p in range(1, 8):
        z_col(p).wait_send()
        z_row(p).wait_send()
    for c in (col_to_sib, row_to_nbr, colf_to_sib, colf_to_nbr, gimg_to_nbr, rowabs_to_sib, gtxt_to_nbr):
        c.wait_send()
    gtxt_to_nbr.wait_recv()
    otxt_ref[...] = logit_scale * gtxt[ROWS:] + grecv[1].astype(jnp.float32)


def local(image_emb, text_emb, labels):
    width = image_emb.shape[1]
    bf16, f32 = jnp.bfloat16, jnp.float32
    dma = pltpu.SemaphoreType.DMA
    block = jax.ShapeDtypeStruct((ROWS, width), f32)
    return pl.pallas_call(
        kernel,
        out_shape=(block, block),
        in_specs=[
            pl.BlockSpec(memory_space=pl.ANY),
            pl.BlockSpec(memory_space=pl.ANY),
            pl.BlockSpec(memory_space=pltpu.VMEM),
        ],
        out_specs=(pl.BlockSpec(memory_space=pltpu.VMEM), pl.BlockSpec(memory_space=pltpu.VMEM)),
        scratch_shapes=[
            pltpu.VMEM((PLANES, 2, ROWS, width), bf16),
            pltpu.VMEM((PLANES, 2, ROWS, width), bf16),
            pltpu.VMEM((2, ROWS, width), bf16),
            pltpu.VMEM((2, ROWS, width), bf16),
            pltpu.VMEM((PLANES, 2 * ROWS, 2 * ROWS), f32),
            pltpu.VMEM((2 * ROWS, width), f32),
            pltpu.VMEM((2 * ROWS, width), f32),
            pltpu.VMEM((2, ROWS, width), bf16),
            pltpu.VMEM((2, ROWS, width), bf16),
            pltpu.VMEM((2, PLANES, 1, ROWS), f32),
            pltpu.VMEM((PLANES, 1, ROWS), f32),
            pltpu.VMEM((PLANES, 1, ROWS), f32),
            pltpu.VMEM((PLANES, PLANES, 1, ROWS), f32),
            pltpu.VMEM((2, PLANES, 1, ROWS), f32),
            pltpu.VMEM((1, 1, ROWS), f32),
            pltpu.VMEM((2, 1, ROWS), f32),
            pltpu.VMEM((2, 1, ROWS), f32),
            pltpu.VMEM((2, PLANES, 1, ROWS), f32),
            pltpu.VMEM((2 * ROWS, ROWS), f32),
            pltpu.VMEM((2 * ROWS, ROWS), f32),
            dma((64,)),
            dma((64,)),
            dma((20,)),
            dma((20,)),
            dma((16,)),
            dma((16,)),
            dma((9,)),
            dma((9,)),
            dma((4,)),
        ],
        compiler_params=pltpu.CompilerParams(
            collective_id=0, has_side_effects=True, vmem_limit_bytes=32 * 1024 * 1024
        ),
        cost_estimate=pl.CostEstimate(
            flops=8 * 8 * 256 * 256 * 512, bytes_accessed=4 * 1024 * 1024, transcendentals=6 * 8 * 256 * 256
        ),
    )(image_emb, text_emb, labels.reshape(1, ROWS))


def solution(mesh):
    rows = P(("rep", "dp"), None)
    return jax.shard_map(
        local,
        mesh=mesh,
        in_specs=(rows, rows, P(("rep", "dp"))),
        out_specs=(rows, rows),
        check_vma=False,
    )
```

```python
import functools
import math

import jax
import jax.numpy as jnp
from jax import lax
from jax.experimental import pallas as pl
from jax.experimental.pallas import tpu as pltpu
from jax.sharding import PartitionSpec as P

logit_scale = 10.0
log2_scale = logit_scale / math.log(2.0)

ROWS = 128
HALF = 64
CHUNKS = (32, 64)
PLANES = 8
MESH = pl.DeviceIdType.MESH

OFFSETS = (0, -1, -2, -3, 1, 2, 3, 4)
SLOT_OF = {o: i for i, o in enumerate(OFFSETS)}
SLOT_OF[-4] = 7


def scores_of(rows, cols):
    return log2_scale * lax.dot_general(
        rows, cols, (((1,), (1,)), ((), ())), preferred_element_type=jnp.float32
    )


def to_lanes(column):
    return jnp.transpose(jnp.broadcast_to(column, (ROWS, ROWS)))[0:1, :]


def to_sublanes(lanes):
    return jnp.transpose(jnp.broadcast_to(lanes, (ROWS, ROWS)))


def log_add(a, b):
    top = jnp.maximum(a, b)
    return top + jnp.log2(jnp.exp2(a - top) + jnp.exp2(b - top))


def kernel(
    img_ref, txt_ref, lab_ref, oimg_ref, otxt_ref, rimg_ref, rtxt_ref,
    cimg, ctxt, rimg, rtxt, scores, tscores, wide, gimg, gtxt, gsend,
    colp, sibrx, chipcol, zrx, colf, colx, rowp, rowrx, rowabs, rsub, csub,
    ring_t, ring_i, sib_r, z_r, misc_s, misc_r, sent, loc_s,
):
    me = lax.axis_index("dp")
    z, x, k = me // 4, (me // 2) % 2, me % 2

    def device(plane, column, core):
        return {"dp": lax.rem(plane + PLANES, PLANES) * 4 + column * 2 + core}

    right, left = device(z + 1, x, k), device(z - 1, x, k)
    nbr, sib = device(z, 1 - x, k), device(z, x, 1 - k)
    held = (ctxt, cimg)
    rows_of = (rtxt, rimg)
    given = (txt_ref, img_ref)

    def remote(src, dst, send, recv, to):
        return pltpu.make_async_remote_copy(
            src_ref=src, dst_ref=dst, send_sem=send, recv_sem=recv, device_id=to, device_id_type=MESH
        )

    def plane_of(slot):
        off = OFFSETS[slot] if isinstance(slot, int) else jnp.where(slot < 4, -slot, slot - 3)
        return lax.rem(z + off + PLANES, PLANES)

    def slot(d, s):
        return 0 if s == 0 else 7 if s == 4 else s + 3 * d

    def chunks(a, d, s):
        every = range(ROWS // CHUNKS[a])
        return [c for c in every if s < 4 or (c * CHUNKS[a] < HALF) == (d == 0)]

    def ring_id(a, d, s, c):
        before = [(e, t, b) for e in range(2) for t in range(1, 5) for b in chunks(a, e, t)]
        return before.index((d, s, c))

    def ring(a, d, s, c):
        part = pl.ds(c * CHUNKS[a], CHUNKS[a])
        src = given[a].at[part] if s == 1 else held[a].at[slot(d, s - 1), 0, part]
        arrived = (ring_t, ring_i)[a].at[ring_id(a, d, s, c)]
        return remote(src, held[a].at[slot(d, s), 0, part], sent.at[a], arrived, (right, left)[d])

    def to_sib(a, d, s):
        i = (a * 2 + d) * 5 + s
        if s == 0:
            src, dst = given[a], held[a].at[0, 1]
        elif s == 4:
            part = pl.ds(HALF * d, HALF)
            src, dst = held[a].at[7, 0, part], held[a].at[7, 1, part]
        else:
            src, dst = held[a].at[slot(d, s), 0], held[a].at[slot(d, s), 1]
        return remote(src, dst, sent.at[2 + a], sib_r.at[i], sib)

    def misc(i, src, dst, to):
        return remote(src, dst, misc_s.at[i], misc_r.at[i], to)

    def rows_to_nbr(a):
        return misc(a, given[a], rows_of[a].at[0], nbr)

    def z_col(p):
        return remote(
            chipcol, zrx.at[SLOT_OF[-OFFSETS[p]] - 1], sent.at[4], z_r.at[0],
            device(z + OFFSETS[p], x, k),
        )

    def z_row(p):
        return remote(
            rowabs.at[0, z], rowabs.at[0, z], sent.at[5], z_r.at[1],
            device(z + OFFSETS[p], x, k),
        )

    def all_bytes(ref, sem):
        pltpu.make_async_copy(ref, ref, sem).wait()

    own = [
        pltpu.make_async_copy(given[0], ctxt.at[0, 0], loc_s.at[0]),
        pltpu.make_async_copy(given[1], rimg.at[1], loc_s.at[1]),
        pltpu.make_async_copy(given[1], cimg.at[0, 0], loc_s.at[2]),
        pltpu.make_async_copy(given[0], rtxt.at[1], loc_s.at[3]),
    ]
    for c in own:
        c.start()
    barrier = pltpu.get_barrier_semaphore()
    peers = [right, left, nbr, sib]
    for p in peers:
        pl.semaphore_signal(barrier, inc=1, device_id=p, device_id_type=MESH)
    pl.semaphore_wait(barrier, len(peers))

    def first_sends_paced(a):
        def pair(c):
            for d in range(2):
                ring(a, d, 1, c).start()

        return [functools.partial(pair, c) for c in chunks(a, 0, 1)]

    def first_sends(a):
        for c in chunks(a, 0, 1):
            for d in range(2):
                ring(a, d, 1, c).start()

    def ring_step(a, s, beside=()):
        beside = list(beside)
        for c in chunks(a, 0, 1):
            for d in range(2):
                if c in chunks(a, d, s):
                    ring(a, d, s, c).wait_recv()
                    if s < 4 and c in chunks(a, d, s + 1):
                        ring(a, d, s + 1, c).start()
            if beside:
                beside.pop(0)()
        for thunk in beside:
            thunk()
        for d in range(2):
            to_sib(a, d, s).start()

    def from_sib(a, s):
        for d in range(2):
            to_sib(a, d, s).wait_recv()

    first_sends(0)
    to_sib(0, 0, 0).start()
    rows_to_nbr(1).start()

    row_peak = jnp.full((2 * ROWS, 1), -jnp.inf, jnp.float32)
    row_mass = jnp.zeros((2 * ROWS, 1), jnp.float32)

    def image_tile(q, peak, mass):
        s = scores_of(rimg[...].reshape(2 * ROWS, -1), ctxt[q].reshape(2 * ROWS, -1))
        scores[q] = s
        top = jnp.max(s, axis=0, keepdims=True)
        col = top + jnp.log2(jnp.sum(jnp.exp2(s - top), axis=0, keepdims=True))
        for kr in range(2):
            colp[kr, plane_of(q)] = col[:, kr * ROWS : (kr + 1) * ROWS]
        new_peak = jnp.maximum(peak, jnp.max(s, axis=1, keepdims=True))
        mass = mass * jnp.exp2(peak - new_peak) + jnp.sum(jnp.exp2(s - new_peak), axis=1, keepdims=True)
        return new_peak, mass

    def text_tile(q):
        tscores[q] = scores_of(rtxt[...].reshape(2 * ROWS, -1), cimg[q].reshape(2 * ROWS, -1))

    ring_step(0, 1)
    own[0].wait()
    own[1].wait()
    rows_to_nbr(1).wait_recv()
    to_sib(0, 0, 0).wait_recv()
    row_peak, row_mass = image_tile(0, row_peak, row_mass)
    ring_step(0, 2)
    first_sends(1)
    to_sib(1, 0, 0).start()
    rows_to_nbr(0).start()
    from_sib(0, 1)
    for q in (1, 4):
        row_peak, row_mass = image_tile(q, row_peak, row_mass)
    ring_step(0, 3)
    from_sib(0, 2)
    for q in (2, 5):
        row_peak, row_mass = image_tile(q, row_peak, row_mass)
    ring_step(0, 4)
    ring_step(1, 1)
    from_sib(0, 3)
    for q in (3, 6):
        row_peak, row_mass = image_tile(q, row_peak, row_mass)
    from_sib(0, 4)
    row_peak, row_mass = image_tile(7, row_peak, row_mass)

    col_to_sib = misc(2, colp.at[1], sibrx, sib)
    col_to_sib.start()
    row_part = row_peak + jnp.log2(row_mass)
    rowp[0] = to_lanes(row_part[:ROWS])
    rowp[1] = to_lanes(row_part[ROWS:])
    row_to_nbr = misc(3, rowp, rowrx, nbr)
    row_to_nbr.start()
    col_to_sib.wait_recv()
    chipcol[...] = log_add(colp[0], sibrx[...])
    for p in range(1, 8):
        z_col(p).start()
    ring_step(1, 2)
    own[2].wait()
    own[3].wait()
    rows_to_nbr(0).wait_recv()
    to_sib(1, 0, 0).wait_recv()
    text_tile(0)
    row_to_nbr.wait_recv()
    row_nbr = log_add(rowp[0], rowrx[1])
    row_own = log_add(rowp[1], rowrx[0])
    rowabs[0, z] = row_own
    for p in range(1, 8):
        z_row(p).start()
    rsub[:ROWS] = to_sublanes(row_nbr + 1.0)
    rsub[ROWS:] = to_sublanes(row_own + 1.0)
    from_sib(1, 1)
    text_tile(1)
    text_tile(4)
    ring_step(1, 3)
    from_sib(1, 2)
    text_tile(2)
    text_tile(5)
    all_bytes(zrx, z_r.at[0])
    parts = [chipcol[...]] + [zrx[p] for p in range(7)]
    top = functools.reduce(jnp.maximum, parts)
    mass = sum(jnp.exp2(p - top) for p in parts)
    colf[0] = top + jnp.log2(mass)
    colf_to_sib = misc(4, colf.at[0], colf.at[1], sib)
    colf_to_sib.start()
    colf_to_nbr = misc(5, colf.at[0, z], colx.at[0], nbr)
    colf_to_nbr.start()
    all_bytes(rowabs.at[0, pl.ds(0, 7)], z_r.at[1])
    rowabs_to_sib = misc(7, rowabs.at[0], rowabs.at[1], sib)
    rowabs_to_sib.start()
    colf_to_sib.wait_recv()

    def lanes_of(ref, q):
        plane = plane_of(q)
        return jnp.concatenate([ref[0, plane], ref[1, plane]], axis=1) + 1.0

    def weights_of(s, sub, lanes):
        return jnp.exp2(s - jnp.concatenate([sub, sub], axis=1)) + jnp.exp2(s - lanes)

    def with_positive(w, positive):
        zero = jnp.zeros((ROWS, ROWS), jnp.float32)
        mask = jnp.concatenate([zero, positive.astype(jnp.float32)], axis=0)
        return w - jnp.concatenate([mask, jnp.zeros((2 * ROWS, ROWS), jnp.float32)], axis=1)

    labels = lab_ref[...] - me * ROWS
    label_rows = to_sublanes(labels.astype(jnp.float32))
    lane_ids = lax.broadcasted_iota(jnp.int32, (ROWS, ROWS), 1)
    row_ids = lax.broadcasted_iota(jnp.int32, (ROWS, ROWS), 0)

    def image_weights(q):
        return weights_of(scores[q], rsub[...], lanes_of(colf, q))

    def place(q, w):
        wide[:, q * 2 * ROWS : (q + 1) * 2 * ROWS] = w.astype(jnp.bfloat16)

    place(0, with_positive(image_weights(0), label_rows == lane_ids.astype(jnp.float32)))
    for q in range(1, 8):
        place(q, image_weights(q))
    gimg[...] = logit_scale * jnp.dot(
        wide[...], ctxt[...].reshape(8 * 2 * ROWS, -1), preferred_element_type=jnp.float32
    )
    gsend[0] = gimg[:ROWS].astype(jnp.bfloat16)
    gimg_to_nbr = misc(6, gsend.at[0], rimg_ref, nbr)
    gimg_to_nbr.start()
    oimg_ref[...] = gimg[ROWS:]

    ring_step(1, 4)
    colf_to_nbr.wait_recv()
    csub[:ROWS] = to_sublanes(colx[0] + 1.0)
    csub[ROWS:] = to_sublanes(colf[0, z] + 1.0)
    from_sib(1, 3)
    text_tile(3)
    text_tile(6)
    rowabs_to_sib.wait_recv()

    def text_weights(q):
        return weights_of(tscores[q], csub[...], lanes_of(rowabs, q))

    place(0, with_positive(text_weights(0), labels == row_ids))
    for q in range(1, 7):
        place(q, text_weights(q))
    gtxt[...] = jnp.dot(
        wide[:, : 7 * 2 * ROWS], cimg[:7].reshape(7 * 2 * ROWS, -1), preferred_element_type=jnp.float32
    )
    from_sib(1, 4)
    text_tile(7)
    last = jnp.dot(
        text_weights(7).astype(jnp.bfloat16), cimg[7].reshape(2 * ROWS, -1), preferred_element_type=jnp.float32
    )
    gtxt[...] = logit_scale * (gtxt[...] + last)
    gsend[1] = gtxt[:ROWS].astype(jnp.bfloat16)
    gtxt_to_nbr = misc(8, gsend.at[1], rtxt_ref, nbr)
    gtxt_to_nbr.start()

    otxt_ref[...] = gtxt[ROWS:]

    for a in range(2):
        all_bytes(held[a].at[pl.ds(0, 7), 0], sent.at[a])
        all_bytes(held[a].at[:, 0], sent.at[2 + a])
        rows_to_nbr(a).wait_send()
    all_bytes(zrx, sent.at[4])
    all_bytes(rowabs.at[0, pl.ds(0, 7)], sent.at[5])
    for c in (col_to_sib, row_to_nbr, colf_to_sib, colf_to_nbr, gimg_to_nbr, rowabs_to_sib, gtxt_to_nbr):
        c.wait_send()
    gimg_to_nbr.wait_recv()
    gtxt_to_nbr.wait_recv()


def local(image_emb, text_emb, labels):
    width = image_emb.shape[1]
    bf16, f32 = jnp.bfloat16, jnp.float32
    dma = pltpu.SemaphoreType.DMA
    block = jax.ShapeDtypeStruct((ROWS, width), f32)
    other = jax.ShapeDtypeStruct((ROWS, width), bf16)
    own_img, own_txt, nbr_img, nbr_txt = pl.pallas_call(
        kernel,
        out_shape=(block, block, other, other),
        in_specs=[
            pl.BlockSpec(memory_space=pl.ANY),
            pl.BlockSpec(memory_space=pl.ANY),
            pl.BlockSpec(memory_space=pltpu.VMEM),
        ],
        out_specs=(pl.BlockSpec(memory_space=pltpu.VMEM),) * 4,
        scratch_shapes=[
            pltpu.VMEM((PLANES, 2, ROWS, width), bf16),
            pltpu.VMEM((PLANES, 2, ROWS, width), bf16),
            pltpu.VMEM((2, ROWS, width), bf16),
            pltpu.VMEM((2, ROWS, width), bf16),
            pltpu.VMEM((PLANES, 2 * ROWS, 2 * ROWS), f32),
            pltpu.VMEM((PLANES, 2 * ROWS, 2 * ROWS), f32),
            pltpu.VMEM((2 * ROWS, PLANES * 2 * ROWS), bf16),
            pltpu.VMEM((2 * ROWS, width), f32),
            pltpu.VMEM((2 * ROWS, width), f32),
            pltpu.VMEM((2, ROWS, width), bf16),
            pltpu.VMEM((2, PLANES, 1, ROWS), f32),
            pltpu.VMEM((PLANES, 1, ROWS), f32),
            pltpu.VMEM((PLANES, 1, ROWS), f32),
            pltpu.VMEM((PLANES - 1, PLANES, 1, ROWS), f32),
            pltpu.VMEM((2, PLANES, 1, ROWS), f32),
            pltpu.VMEM((1, 1, ROWS), f32),
            pltpu.VMEM((2, 1, ROWS), f32),
            pltpu.VMEM((2, 1, ROWS), f32),
            pltpu.VMEM((2, PLANES, 1, ROWS), f32),
            pltpu.VMEM((2 * ROWS, ROWS), f32),
            pltpu.VMEM((2 * ROWS, ROWS), f32),
            dma((7 * ROWS // CHUNKS[0],)),
            dma((7 * ROWS // CHUNKS[1],)),
            dma((20,)),
            dma((2,)),
            dma((9,)),
            dma((9,)),
            dma((6,)),
            dma((4,)),
        ],
        compiler_params=pltpu.CompilerParams(
            collective_id=0, has_side_effects=True, vmem_limit_bytes=32 * 1024 * 1024
        ),
        cost_estimate=pl.CostEstimate(
            flops=8 * 8 * 256 * 256 * 512, bytes_accessed=4 * 1024 * 1024, transcendentals=6 * 8 * 256 * 256
        ),
    )(image_emb, text_emb, labels.reshape(1, ROWS))
    return own_img + nbr_img.astype(f32), own_txt + nbr_txt.astype(f32)


def solution(mesh):
    rows = P(("rep", "dp"), None)
    return jax.shard_map(
        local,
        mesh=mesh,
        in_specs=(rows, rows, P(("rep", "dp"))),
        out_specs=(rows, rows),
        check_vma=False,
    )
```

```python
import functools
import math

import jax
import jax.numpy as jnp
from jax import lax
from jax.experimental import pallas as pl
from jax.experimental.pallas import tpu as pltpu
from jax.sharding import PartitionSpec as P

logit_scale = 10.0
log2_scale = logit_scale / math.log(2.0)

ROWS = 128
HALF = 64
CHUNKS = (32, 32)
PLANES = 8
MESH = pl.DeviceIdType.MESH

OFFSETS = (0, -1, -2, -3, 1, 2, 3, 4)
SLOT_OF = {o: i for i, o in enumerate(OFFSETS)}
SLOT_OF[-4] = 7


def scores_of(rows, cols):
    return log2_scale * lax.dot_general(
        rows, cols, (((1,), (1,)), ((), ())), preferred_element_type=jnp.float32
    )


def to_lanes(column):
    return jnp.transpose(jnp.broadcast_to(column, (ROWS, ROWS)))[0:1, :]


def to_sublanes(lanes):
    return jnp.transpose(jnp.broadcast_to(lanes, (ROWS, ROWS)))


def log_add(a, b):
    top = jnp.maximum(a, b)
    return top + jnp.log2(jnp.exp2(a - top) + jnp.exp2(b - top))


def kernel(
    both_ref, lab_ref, oimg_ref, otxt_ref, rimg_ref, rtxt_ref,
    cimg, ctxt, rimg, rtxt, scores, tscores, wide, gimg, gtxt, gsend,
    colp, sibrx, zmsg, zrx, drx, final, colx, rowp, rowrx, rsub, csub,
    ring_t, ring_i, sib_r, z_r, misc_s, misc_r, sent, loc_s,
):
    me = lax.axis_index("dp")
    z, x, k = me // 4, (me // 2) % 2, me % 2

    def device(plane, column, core):
        return {"dp": lax.rem(plane + PLANES, PLANES) * 4 + column * 2 + core}

    right, left = device(z + 1, x, k), device(z - 1, x, k)
    nbr, sib = device(z, 1 - x, k), device(z, x, 1 - k)
    held = (ctxt, cimg)
    rows_of = (rtxt, rimg)
    given = (both_ref.at[1], both_ref.at[0])

    def remote(src, dst, send, recv, to):
        return pltpu.make_async_remote_copy(
            src_ref=src, dst_ref=dst, send_sem=send, recv_sem=recv, device_id=to, device_id_type=MESH
        )

    def plane_of(slot):
        off = OFFSETS[slot] if isinstance(slot, int) else jnp.where(slot < 4, -slot, slot - 3)
        return lax.rem(z + off + PLANES, PLANES)

    def slot(d, s):
        return 0 if s == 0 else 7 if s == 4 else s + 3 * d

    def chunks(a, d, s):
        every = range(ROWS // CHUNKS[a])
        return [c for c in every if s < 4 or (c * CHUNKS[a] < HALF) == (d == 0)]

    def ring_id(a, d, s, c):
        before = [(e, t, b) for e in range(2) for t in range(1, 5) for b in chunks(a, e, t)]
        return before.index((d, s, c))

    def ring(a, d, s, c):
        part = pl.ds(c * CHUNKS[a], CHUNKS[a])
        src = given[a].at[part] if s == 1 else held[a].at[slot(d, s - 1), 0, part]
        arrived = (ring_t, ring_i)[a].at[ring_id(a, d, s, c)]
        return remote(src, held[a].at[slot(d, s), 0, part], sent.at[a], arrived, (right, left)[d])

    def to_sib(a, d, s):
        if s == 0:
            src, dst = given[a], held[a].at[0, 1]
        elif s == 4:
            part = pl.ds(HALF * d, HALF)
            src, dst = held[a].at[7, 0, part], held[a].at[7, 1, part]
        else:
            src, dst = held[a].at[slot(d, s), 0], held[a].at[slot(d, s), 1]
        return remote(src, dst, sent.at[2 + a], sib_r.at[a * 5 + s], sib)

    def misc(i, src, dst, to):
        return remote(src, dst, misc_s.at[i], misc_r.at[i], to)

    def rows_to_nbr(a):
        return misc(a, given[a], rows_of[a].at[0], nbr)

    def z_sums(p):
        there = SLOT_OF[-OFFSETS[p]] - 1
        return remote(zmsg, zrx.at[there], sent.at[4], z_r.at[0], device(z + OFFSETS[p], x, k))

    def z_rows(p):
        there = SLOT_OF[-OFFSETS[p]] - 1
        return remote(rowp.at[0], drx.at[there], sent.at[5], z_r.at[1], device(z + OFFSETS[p], 1 - x, k))

    def all_bytes(ref, sem):
        pltpu.make_async_copy(ref, ref, sem).wait()

    own = [
        pltpu.make_async_copy(given[0], ctxt.at[0, 0], loc_s.at[0]),
        pltpu.make_async_copy(given[1], rimg.at[1], loc_s.at[1]),
        pltpu.make_async_copy(given[1], cimg.at[0, 0], loc_s.at[2]),
        pltpu.make_async_copy(given[0], rtxt.at[1], loc_s.at[3]),
    ]
    barrier = pltpu.get_barrier_semaphore()
    peers = [right, left, nbr, sib]
    for p in peers:
        pl.semaphore_signal(barrier, inc=1, device_id=p, device_id_type=MESH)
    pl.semaphore_wait(barrier, len(peers))

    def first_sends(a):
        for c in chunks(a, 0, 1):
            for d in range(2):
                ring(a, d, 1, c).start()

    def step_thunks(a, s):
        def one(c):
            for d in range(2):
                if c in chunks(a, d, s):
                    ring(a, d, s, c).wait_recv()
                    if s < 4 and c in chunks(a, d, s + 1):
                        ring(a, d, s + 1, c).start()

        return [functools.partial(one, c) for c in chunks(a, 0, 1)]

    def ring_step(a, s, beside=()):
        beside = list(beside)
        for c in chunks(a, 0, 1):
            for d in range(2):
                if c in chunks(a, d, s):
                    ring(a, d, s, c).wait_recv()
                    if s < 4 and c in chunks(a, d, s + 1):
                        ring(a, d, s + 1, c).start()
            if beside:
                beside.pop(0)()
        for thunk in beside:
            thunk()
        for d in range(2):
            to_sib(a, d, s).start()

    def from_sib(a, s):
        if s == 4:
            all_bytes(held[a].at[7, 1], sib_r.at[a * 5 + 4])
        else:
            all_bytes(held[a].at[pl.ds(0, 2), 1], sib_r.at[a * 5 + s])

    first_sends(0)
    to_sib(0, 0, 0).start()
    rows_to_nbr(1).start()
    for c in own:
        c.start()

    row_peak = jnp.full((2 * ROWS, 1), -jnp.inf, jnp.float32)
    row_mass = jnp.zeros((2 * ROWS, 1), jnp.float32)

    def image_tile(q, peak, mass):
        s = scores_of(rimg[...].reshape(2 * ROWS, -1), ctxt[q].reshape(2 * ROWS, -1))
        scores[q] = s
        top = jnp.max(s, axis=0, keepdims=True)
        col = top + jnp.log2(jnp.sum(jnp.exp2(s - top), axis=0, keepdims=True))
        for kr in range(2):
            colp[kr, plane_of(q)] = col[:, kr * ROWS : (kr + 1) * ROWS]
        new_peak = jnp.maximum(peak, jnp.max(s, axis=1, keepdims=True))
        mass = mass * jnp.exp2(peak - new_peak) + jnp.sum(jnp.exp2(s - new_peak), axis=1, keepdims=True)
        return new_peak, mass

    def text_tile(q):
        tscores[q] = scores_of(rtxt[...].reshape(2 * ROWS, -1), cimg[q].reshape(2 * ROWS, -1))

    ring_step(0, 1)
    own[0].wait()
    own[1].wait()
    rows_to_nbr(1).wait_recv()
    to_sib(0, 0, 0).wait_recv()
    row_peak, row_mass = image_tile(0, row_peak, row_mass)
    ring_step(0, 2)
    first_sends(1)
    to_sib(1, 0, 0).start()
    rows_to_nbr(0).start()
    from_sib(0, 1)
    for q in (1, 4):
        row_peak, row_mass = image_tile(q, row_peak, row_mass)
    ring_step(0, 3)
    from_sib(0, 2)
    for q in (2, 5):
        row_peak, row_mass = image_tile(q, row_peak, row_mass)
    from_sib(0, 3)
    for q in (3, 6):
        row_peak, row_mass = image_tile(q, row_peak, row_mass)
    ring_step(0, 4, step_thunks(1, 1))
    for d in range(2):
        to_sib(1, d, 1).start()
    from_sib(0, 4)
    row_peak, row_mass = image_tile(7, row_peak, row_mass)

    col_to_sib = misc(2, colp.at[1], sibrx, sib)
    col_to_sib.start()
    row_part = row_peak + jnp.log2(row_mass)
    rowp[0] = to_lanes(row_part[:ROWS])
    rowp[1] = to_lanes(row_part[ROWS:])
    zmsg[8] = rowp[1]
    row_to_nbr = misc(3, rowp, rowrx, nbr)
    row_to_nbr.start()
    col_to_sib.wait_recv()
    zmsg[:8] = log_add(colp[0], sibrx[...])
    for p in range(1, 8):
        z_sums(p).start()
    for p in range(1, 8):
        z_rows(p).start()
    ring_step(1, 2)
    own[2].wait()
    own[3].wait()
    rows_to_nbr(0).wait_recv()
    to_sib(1, 0, 0).wait_recv()
    text_tile(0)
    row_to_nbr.wait_recv()
    row_nbr = log_add(rowp[0], rowrx[1])
    row_own = log_add(rowp[1], rowrx[0])
    final[0, 8 + z] = row_own
    rsub[:ROWS] = to_sublanes(row_nbr + 1.0)
    rsub[ROWS:] = to_sublanes(row_own + 1.0)
    from_sib(1, 1)
    text_tile(1)
    text_tile(4)
    ring_step(1, 3)
    from_sib(1, 2)
    text_tile(2)
    text_tile(5)
    all_bytes(zrx, z_r.at[0])
    all_bytes(drx, z_r.at[1])
    parts = [zmsg[:8]] + [zrx[p, :8] for p in range(7)]
    top = functools.reduce(jnp.maximum, parts)
    mass = sum(jnp.exp2(p - top) for p in parts)
    final[0, :8] = top + jnp.log2(mass)
    for p in range(1, 8):
        final[0, 8 + plane_of(p)] = log_add(zrx[p - 1, 8], drx[p - 1])
    final_to_sib = misc(4, final.at[0], final.at[1], sib)
    final_to_sib.start()
    col_to_nbr = misc(5, final.at[0, z], colx.at[0], nbr)
    col_to_nbr.start()
    final_to_sib.wait_recv()

    def lanes_of(side, q):
        plane = 8 * side + plane_of(q)
        return jnp.concatenate([final[0, plane], final[1, plane]], axis=1) + 1.0

    def weights_of(s, sub, lanes):
        return jnp.exp2(s - jnp.concatenate([sub, sub], axis=1)) + jnp.exp2(s - lanes)

    def with_positive(w, positive):
        zero = jnp.zeros((ROWS, ROWS), jnp.float32)
        mask = jnp.concatenate([zero, positive.astype(jnp.float32)], axis=0)
        return w - jnp.concatenate([mask, jnp.zeros((2 * ROWS, ROWS), jnp.float32)], axis=1)

    labels = lab_ref[...] - me * ROWS
    label_rows = to_sublanes(labels.astype(jnp.float32))
    lane_ids = lax.broadcasted_iota(jnp.int32, (ROWS, ROWS), 1)
    row_ids = lax.broadcasted_iota(jnp.int32, (ROWS, ROWS), 0)

    def image_weights(q):
        return weights_of(scores[q], rsub[...], lanes_of(0, q))

    def place(q, w):
        wide[:, q * 2 * ROWS : (q + 1) * 2 * ROWS] = w.astype(jnp.bfloat16)

    place(0, with_positive(image_weights(0), label_rows == lane_ids.astype(jnp.float32)))
    for q in range(1, 8):
        place(q, image_weights(q))
    gimg[...] = logit_scale * jnp.dot(
        wide[...], ctxt[...].reshape(8 * 2 * ROWS, -1), preferred_element_type=jnp.float32
    )
    gsend[0] = gimg[:ROWS].astype(jnp.bfloat16)
    gimg_to_nbr = misc(6, gsend.at[0], rimg_ref, nbr)
    gimg_to_nbr.start()
    oimg_ref[...] = gimg[ROWS:]

    for d in range(2):
        for c in chunks(1, d, 4):
            ring(1, d, 4, c).wait_recv()
        to_sib(1, d, 4).start()
    col_to_nbr.wait_recv()
    csub[:ROWS] = to_sublanes(colx[0] + 1.0)
    csub[ROWS:] = to_sublanes(final[0, z] + 1.0)
    from_sib(1, 3)
    text_tile(3)
    text_tile(6)

    def text_weights(q):
        return weights_of(tscores[q], csub[...], lanes_of(1, q))

    place(0, with_positive(text_weights(0), labels == row_ids))
    for q in range(1, 7):
        place(q, text_weights(q))
    gtxt[...] = jnp.dot(
        wide[:, : 7 * 2 * ROWS], cimg[:7].reshape(7 * 2 * ROWS, -1), preferred_element_type=jnp.float32
    )
    from_sib(1, 4)
    text_tile(7)
    last = jnp.dot(
        text_weights(7).astype(jnp.bfloat16), cimg[7].reshape(2 * ROWS, -1), preferred_element_type=jnp.float32
    )
    gtxt[...] = logit_scale * (gtxt[...] + last)
    gsend[1] = gtxt[:ROWS].astype(jnp.bfloat16)
    gtxt_to_nbr = misc(7, gsend.at[1], rtxt_ref, nbr)
    gtxt_to_nbr.start()

    otxt_ref[...] = gtxt[ROWS:]

    for a in range(2):
        all_bytes(held[a].at[pl.ds(0, 7), 0], sent.at[a])
        all_bytes(held[a].at[:, 0], sent.at[2 + a])
        rows_to_nbr(a).wait_send()
    all_bytes(zrx, sent.at[4])
    all_bytes(drx, sent.at[5])
    for c in (col_to_sib, row_to_nbr, final_to_sib, col_to_nbr, gimg_to_nbr, gtxt_to_nbr):
        c.wait_send()
    gimg_to_nbr.wait_recv()
    gtxt_to_nbr.wait_recv()


def local(image_emb, text_emb, labels):
    width = image_emb.shape[1]
    bf16, f32 = jnp.bfloat16, jnp.float32
    dma = pltpu.SemaphoreType.DMA
    block = jax.ShapeDtypeStruct((ROWS, width), f32)
    other = jax.ShapeDtypeStruct((ROWS, width), bf16)
    own_img, own_txt, nbr_img, nbr_txt = pl.pallas_call(
        kernel,
        out_shape=(block, block, other, other),
        in_specs=[
            pl.BlockSpec(memory_space=pl.ANY),
            pl.BlockSpec(memory_space=pltpu.VMEM),
        ],
        out_specs=(pl.BlockSpec(memory_space=pltpu.VMEM),) * 4,
        scratch_shapes=[
            pltpu.VMEM((PLANES, 2, ROWS, width), bf16),
            pltpu.VMEM((PLANES, 2, ROWS, width), bf16),
            pltpu.VMEM((2, ROWS, width), bf16),
            pltpu.VMEM((2, ROWS, width), bf16),
            pltpu.VMEM((PLANES, 2 * ROWS, 2 * ROWS), f32),
            pltpu.VMEM((PLANES, 2 * ROWS, 2 * ROWS), f32),
            pltpu.VMEM((2 * ROWS, PLANES * 2 * ROWS), bf16),
            pltpu.VMEM((2 * ROWS, width), f32),
            pltpu.VMEM((2 * ROWS, width), f32),
            pltpu.VMEM((2, ROWS, width), bf16),
            pltpu.VMEM((2, PLANES, 1, ROWS), f32),
            pltpu.VMEM((PLANES, 1, ROWS), f32),
            pltpu.VMEM((PLANES + 1, 1, ROWS), f32),
            pltpu.VMEM((PLANES - 1, PLANES + 1, 1, ROWS), f32),
            pltpu.VMEM((PLANES - 1, 1, ROWS), f32),
            pltpu.VMEM((2, 2 * PLANES, 1, ROWS), f32),
            pltpu.VMEM((1, 1, ROWS), f32),
            pltpu.VMEM((2, 1, ROWS), f32),
            pltpu.VMEM((2, 1, ROWS), f32),
            pltpu.VMEM((2 * ROWS, ROWS), f32),
            pltpu.VMEM((2 * ROWS, ROWS), f32),
            dma((7 * ROWS // CHUNKS[0],)),
            dma((7 * ROWS // CHUNKS[1],)),
            dma((10,)),
            dma((2,)),
            dma((8,)),
            dma((8,)),
            dma((6,)),
            dma((4,)),
        ],
        compiler_params=pltpu.CompilerParams(
            collective_id=0, has_side_effects=True, vmem_limit_bytes=32 * 1024 * 1024
        ),
        cost_estimate=pl.CostEstimate(
            flops=8 * 8 * 256 * 256 * 512, bytes_accessed=4 * 1024 * 1024, transcendentals=6 * 8 * 256 * 256
        ),
    )(jnp.stack([image_emb, text_emb]), labels.reshape(1, ROWS))
    return own_img + nbr_img.astype(f32), own_txt + nbr_txt.astype(f32)


def solution(mesh):
    rows = P(("rep", "dp"), None)
    return jax.shard_map(
        local,
        mesh=mesh,
        in_specs=(rows, rows, P(("rep", "dp"))),
        out_specs=(rows, rows),
        check_vma=False,
    )
```

```python
import functools
import math

import jax
import jax.numpy as jnp
from jax import lax
from jax.experimental import pallas as pl
from jax.experimental.pallas import tpu as pltpu
from jax.sharding import PartitionSpec as P

logit_scale = 10.0
log2_scale = logit_scale / math.log(2.0)

ROWS = 128
HALF = 64
CHUNKS = (32, 32)
PLANES = 8
MESH = pl.DeviceIdType.MESH

OFFSETS = (0, -1, -2, -3, 1, 2, 3, 4)
SLOT_OF = {o: i for i, o in enumerate(OFFSETS)}
SLOT_OF[-4] = 7


def scores_of(rows, cols):
    return log2_scale * lax.dot_general(
        rows, cols, (((1,), (1,)), ((), ())), preferred_element_type=jnp.float32
    )


def to_lanes(column):
    return jnp.transpose(jnp.broadcast_to(column, (ROWS, ROWS)))[0:1, :]


def to_sublanes(lanes):
    return jnp.transpose(jnp.broadcast_to(lanes, (ROWS, ROWS)))


def log_add(a, b):
    top = jnp.maximum(a, b)
    return top + jnp.log2(jnp.exp2(a - top) + jnp.exp2(b - top))


def kernel(
    both_ref, lab_ref, oimg_ref, otxt_ref, rimg_ref, rtxt_ref,
    cimg, ctxt, rimg, rtxt, scores, tscores, wide, gtxt, gsend,
    colp, sibrx, zmsg, zrx, drx, final, colx, rowp, rowrx, rsub, csub,
    ring_t, ring_i, sib_r, z_r, misc_s, misc_r, sent, loc_s,
):
    me = lax.axis_index("dp")
    z, x, k = me // 4, (me // 2) % 2, me % 2

    def device(plane, column, core):
        return {"dp": lax.rem(plane + PLANES, PLANES) * 4 + column * 2 + core}

    right, left = device(z + 1, x, k), device(z - 1, x, k)
    nbr, sib = device(z, 1 - x, k), device(z, x, 1 - k)
    held = (ctxt, cimg)
    rows_of = (rtxt, rimg)
    given = (both_ref.at[1], both_ref.at[0])

    def remote(src, dst, send, recv, to):
        return pltpu.make_async_remote_copy(
            src_ref=src, dst_ref=dst, send_sem=send, recv_sem=recv, device_id=to, device_id_type=MESH
        )

    def plane_of(slot):
        off = OFFSETS[slot] if isinstance(slot, int) else jnp.where(slot < 4, -slot, slot - 3)
        return lax.rem(z + off + PLANES, PLANES)

    def slot(d, s):
        return 0 if s == 0 else 7 if s == 4 else s + 3 * d

    def chunks(a, d, s):
        every = range(ROWS // CHUNKS[a])
        return [c for c in every if s < 4 or (c * CHUNKS[a] < HALF) == (d == 0)]

    def ring_id(a, d, s, c):
        before = [(e, t, b) for e in range(2) for t in range(1, 5) for b in chunks(a, e, t)]
        return before.index((d, s, c))

    def ring(a, d, s, c):
        part = pl.ds(c * CHUNKS[a], CHUNKS[a])
        src = given[a].at[part] if s == 1 else held[a].at[slot(d, s - 1), 0, part]
        arrived = (ring_t, ring_i)[a].at[ring_id(a, d, s, c)]
        return remote(src, held[a].at[slot(d, s), 0, part], sent.at[a], arrived, (right, left)[d])

    def to_sib(a, d, s):
        if s == 0:
            src, dst = given[a], held[a].at[0, 1]
        elif s == 4:
            part = pl.ds(HALF * d, HALF)
            src, dst = held[a].at[7, 0, part], held[a].at[7, 1, part]
        else:
            src, dst = held[a].at[slot(d, s), 0], held[a].at[slot(d, s), 1]
        return remote(src, dst, sent.at[2 + a], sib_r.at[a * 5 + s], sib)

    def misc(i, src, dst, to):
        return remote(src, dst, misc_s.at[i], misc_r.at[i], to)

    def rows_to_nbr(a):
        return misc(a, given[a], rows_of[a].at[0], nbr)

    def z_sums(p):
        there = SLOT_OF[-OFFSETS[p]] - 1
        return remote(zmsg, zrx.at[there], sent.at[4], z_r.at[0], device(z + OFFSETS[p], x, k))

    def z_rows(p):
        there = SLOT_OF[-OFFSETS[p]] - 1
        return remote(rowp.at[0], drx.at[there], sent.at[5], z_r.at[1], device(z + OFFSETS[p], 1 - x, k))

    def all_bytes(ref, sem):
        pltpu.make_async_copy(ref, ref, sem).wait()

    own = [
        pltpu.make_async_copy(given[0], ctxt.at[0, 0], loc_s.at[0]),
        pltpu.make_async_copy(given[1], rimg.at[1], loc_s.at[1]),
        pltpu.make_async_copy(given[1], cimg.at[0, 0], loc_s.at[2]),
        pltpu.make_async_copy(given[0], rtxt.at[1], loc_s.at[3]),
    ]
    barrier = pltpu.get_barrier_semaphore()
    peers = [right, left, nbr, sib]
    for p in peers:
        pl.semaphore_signal(barrier, inc=1, device_id=p, device_id_type=MESH)
    pl.semaphore_wait(barrier, len(peers))

    def first_sends(a):
        for c in chunks(a, 0, 1):
            for d in range(2):
                ring(a, d, 1, c).start()

    def step_thunks(a, s):
        def one(c):
            for d in range(2):
                if c in chunks(a, d, s):
                    ring(a, d, s, c).wait_recv()
                    if s < 4 and c in chunks(a, d, s + 1):
                        ring(a, d, s + 1, c).start()

        return [functools.partial(one, c) for c in chunks(a, 0, 1)]

    def ring_step(a, s, beside=()):
        beside = list(beside)
        for c in chunks(a, 0, 1):
            for d in range(2):
                if c in chunks(a, d, s):
                    ring(a, d, s, c).wait_recv()
                    if s < 4 and c in chunks(a, d, s + 1):
                        ring(a, d, s + 1, c).start()
            if beside:
                beside.pop(0)()
        for thunk in beside:
            thunk()
        for d in range(2):
            to_sib(a, d, s).start()

    def from_sib(a, s):
        if s == 4:
            all_bytes(held[a].at[7, 1], sib_r.at[a * 5 + 4])
        else:
            all_bytes(held[a].at[pl.ds(0, 2), 1], sib_r.at[a * 5 + s])

    first_sends(0)
    to_sib(0, 0, 0).start()
    rows_to_nbr(1).start()
    for c in own:
        c.start()

    row_peak = jnp.full((2 * ROWS, 1), -jnp.inf, jnp.float32)
    row_mass = jnp.zeros((2 * ROWS, 1), jnp.float32)

    def image_tile(q, peak, mass):
        s = scores_of(rimg[...].reshape(2 * ROWS, -1), ctxt[q].reshape(2 * ROWS, -1))
        scores[q] = s
        top = jnp.max(s, axis=0, keepdims=True)
        col = top + jnp.log2(jnp.sum(jnp.exp2(s - top), axis=0, keepdims=True))
        for kr in range(2):
            colp[kr, plane_of(q)] = col[:, kr * ROWS : (kr + 1) * ROWS]
        new_peak = jnp.maximum(peak, jnp.max(s, axis=1, keepdims=True))
        mass = mass * jnp.exp2(peak - new_peak) + jnp.sum(jnp.exp2(s - new_peak), axis=1, keepdims=True)
        return new_peak, mass

    def text_tile(q):
        tscores[q] = scores_of(rtxt[...].reshape(2 * ROWS, -1), cimg[q].reshape(2 * ROWS, -1))

    ring_step(0, 1)
    ring_step(0, 2)
    first_sends(1)
    own[0].wait()
    own[1].wait()
    rows_to_nbr(1).wait_recv()
    to_sib(0, 0, 0).wait_recv()
    row_peak, row_mass = image_tile(0, row_peak, row_mass)
    from_sib(0, 1)
    for q in (1, 4):
        row_peak, row_mass = image_tile(q, row_peak, row_mass)
    ring_step(0, 3)
    to_sib(1, 0, 0).start()
    rows_to_nbr(0).start()
    from_sib(0, 2)
    for q in (2, 5):
        row_peak, row_mass = image_tile(q, row_peak, row_mass)
    from_sib(0, 3)
    for q in (3, 6):
        row_peak, row_mass = image_tile(q, row_peak, row_mass)
    ring_step(0, 4, step_thunks(1, 1))
    for d in range(2):
        to_sib(1, d, 1).start()
    from_sib(0, 4)
    row_peak, row_mass = image_tile(7, row_peak, row_mass)

    col_to_sib = misc(2, colp.at[1], sibrx, sib)
    col_to_sib.start()
    row_part = row_peak + jnp.log2(row_mass)
    rowp[0] = to_lanes(row_part[:ROWS])
    rowp[1] = to_lanes(row_part[ROWS:])
    zmsg[8] = rowp[1]
    row_to_nbr = misc(3, rowp, rowrx, nbr)
    row_to_nbr.start()
    col_to_sib.wait_recv()
    zmsg[:8] = log_add(colp[0], sibrx[...])
    for p in range(1, 8):
        z_sums(p).start()
    for p in range(1, 8):
        z_rows(p).start()
    ring_step(1, 2)
    own[2].wait()
    own[3].wait()
    rows_to_nbr(0).wait_recv()
    to_sib(1, 0, 0).wait_recv()
    text_tile(0)
    row_to_nbr.wait_recv()
    row_nbr = log_add(rowp[0], rowrx[1])
    row_own = log_add(rowp[1], rowrx[0])
    final[0, 8 + z] = row_own
    rsub[:ROWS] = to_sublanes(row_nbr + 1.0)
    rsub[ROWS:] = to_sublanes(row_own + 1.0)
    from_sib(1, 1)
    text_tile(1)
    text_tile(4)
    ring_step(1, 3)
    from_sib(1, 2)
    text_tile(2)
    text_tile(5)
    all_bytes(zrx, z_r.at[0])
    all_bytes(drx, z_r.at[1])
    parts = [zmsg[:8]] + [zrx[p, :8] for p in range(7)]
    top = functools.reduce(jnp.maximum, parts)
    mass = sum(jnp.exp2(p - top) for p in parts)
    final[0, :8] = top + jnp.log2(mass)
    for p in range(1, 8):
        final[0, 8 + plane_of(p)] = log_add(zrx[p - 1, 8], drx[p - 1])
    final_to_sib = misc(4, final.at[0], final.at[1], sib)
    final_to_sib.start()
    col_to_nbr = misc(5, final.at[0, z], colx.at[0], nbr)
    col_to_nbr.start()
    final_to_sib.wait_recv()

    def lanes_of(side, q):
        plane = 8 * side + plane_of(q)
        return jnp.concatenate([final[0, plane], final[1, plane]], axis=1) + 1.0

    def weights_of(s, sub, lanes):
        return jnp.exp2(s - jnp.concatenate([sub, sub], axis=1)) + jnp.exp2(s - lanes)

    def products(half, count, tiles, sub, side, cols, positive=None):
        part = pl.ds(half * ROWS, ROWS)
        for q in range(count):
            w = weights_of(tiles[q, part], sub[part], lanes_of(side, q))
            if positive is not None and q == 0:
                mask = positive.astype(jnp.float32)
                w = w - jnp.concatenate([mask, jnp.zeros_like(mask)], axis=1)
            wide[part, q * 2 * ROWS : (q + 1) * 2 * ROWS] = w.astype(jnp.bfloat16)
        depth = count * 2 * ROWS
        return jnp.dot(
            wide[part, :depth], cols[:count].reshape(depth, -1), preferred_element_type=jnp.float32
        )

    gsend[0] = (logit_scale * products(0, 8, scores, rsub, 0, ctxt)).astype(jnp.bfloat16)
    gimg_to_nbr = misc(6, gsend.at[0], rimg_ref, nbr)
    gimg_to_nbr.start()

    for d in range(2):
        for c in chunks(1, d, 4):
            ring(1, d, 4, c).wait_recv()
        to_sib(1, d, 4).start()
    col_to_nbr.wait_recv()
    csub[:ROWS] = to_sublanes(colx[0] + 1.0)
    csub[ROWS:] = to_sublanes(final[0, z] + 1.0)
    from_sib(1, 3)
    text_tile(3)
    text_tile(6)

    gtxt[...] = products(0, 7, tscores, csub, 1, cimg)
    from_sib(1, 4)
    last = cimg[7].reshape(2 * ROWS, -1)
    w = weights_of(scores_of(rtxt[0], last), csub[:ROWS], lanes_of(1, 7)).astype(jnp.bfloat16)
    gsend[1] = (
        logit_scale * (gtxt[...] + jnp.dot(w, last, preferred_element_type=jnp.float32))
    ).astype(jnp.bfloat16)
    gtxt_to_nbr = misc(7, gsend.at[1], rtxt_ref, nbr)
    gtxt_to_nbr.start()

    labels = lab_ref[...] - me * ROWS
    label_rows = to_sublanes(labels.astype(jnp.float32))
    lane_ids = lax.broadcasted_iota(jnp.int32, (ROWS, ROWS), 1).astype(jnp.float32)
    row_ids = lax.broadcasted_iota(jnp.int32, (ROWS, ROWS), 0)
    text_tile(7)
    oimg_ref[...] = logit_scale * products(1, 8, scores, rsub, 0, ctxt, label_rows == lane_ids)
    otxt_ref[...] = logit_scale * products(1, 8, tscores, csub, 1, cimg, labels == row_ids)

    for a in range(2):
        all_bytes(held[a].at[pl.ds(0, 7), 0], sent.at[a])
        all_bytes(held[a].at[:, 0], sent.at[2 + a])
        rows_to_nbr(a).wait_send()
    all_bytes(zrx, sent.at[4])
    all_bytes(drx, sent.at[5])
    for c in (col_to_sib, row_to_nbr, final_to_sib, col_to_nbr, gimg_to_nbr, gtxt_to_nbr):
        c.wait_send()
    gimg_to_nbr.wait_recv()
    gtxt_to_nbr.wait_recv()


def local(image_emb, text_emb, labels):
    width = image_emb.shape[1]
    bf16, f32 = jnp.bfloat16, jnp.float32
    dma = pltpu.SemaphoreType.DMA
    block = jax.ShapeDtypeStruct((ROWS, width), f32)
    other = jax.ShapeDtypeStruct((ROWS, width), bf16)
    own_img, own_txt, nbr_img, nbr_txt = pl.pallas_call(
        kernel,
        out_shape=(block, block, other, other),
        in_specs=[
            pl.BlockSpec(memory_space=pl.ANY),
            pl.BlockSpec(memory_space=pltpu.VMEM),
        ],
        out_specs=(pl.BlockSpec(memory_space=pltpu.VMEM),) * 4,
        scratch_shapes=[
            pltpu.VMEM((PLANES, 2, ROWS, width), bf16),
            pltpu.VMEM((PLANES, 2, ROWS, width), bf16),
            pltpu.VMEM((2, ROWS, width), bf16),
            pltpu.VMEM((2, ROWS, width), bf16),
            pltpu.VMEM((PLANES, 2 * ROWS, 2 * ROWS), f32),
            pltpu.VMEM((PLANES, 2 * ROWS, 2 * ROWS), f32),
            pltpu.VMEM((2 * ROWS, PLANES * 2 * ROWS), bf16),
            pltpu.VMEM((ROWS, width), f32),
            pltpu.VMEM((2, ROWS, width), bf16),
            pltpu.VMEM((2, PLANES, 1, ROWS), f32),
            pltpu.VMEM((PLANES, 1, ROWS), f32),
            pltpu.VMEM((PLANES + 1, 1, ROWS), f32),
            pltpu.VMEM((PLANES - 1, PLANES + 1, 1, ROWS), f32),
            pltpu.VMEM((PLANES - 1, 1, ROWS), f32),
            pltpu.VMEM((2, 2 * PLANES, 1, ROWS), f32),
            pltpu.VMEM((1, 1, ROWS), f32),
            pltpu.VMEM((2, 1, ROWS), f32),
            pltpu.VMEM((2, 1, ROWS), f32),
            pltpu.VMEM((2 * ROWS, ROWS), f32),
            pltpu.VMEM((2 * ROWS, ROWS), f32),
            dma((7 * ROWS // CHUNKS[0],)),
            dma((7 * ROWS // CHUNKS[1],)),
            dma((10,)),
            dma((2,)),
            dma((8,)),
            dma((8,)),
            dma((6,)),
            dma((4,)),
        ],
        compiler_params=pltpu.CompilerParams(
            collective_id=0, has_side_effects=True, vmem_limit_bytes=32 * 1024 * 1024
        ),
        cost_estimate=pl.CostEstimate(
            flops=8 * 8 * 256 * 256 * 512, bytes_accessed=4 * 1024 * 1024, transcendentals=6 * 8 * 256 * 256
        ),
    )(jnp.stack([image_emb, text_emb]), labels.reshape(1, ROWS))
    return own_img + nbr_img.astype(f32), own_txt + nbr_txt.astype(f32)


def solution(mesh):
    rows = P(("rep", "dp"), None)
    return jax.shard_map(
        local,
        mesh=mesh,
        in_specs=(rows, rows, P(("rep", "dp"))),
        out_specs=(rows, rows),
        check_vma=False,
    )
```

```python
import functools
import math

import jax
import jax.numpy as jnp
from jax import lax
from jax.experimental import pallas as pl
from jax.experimental.pallas import tpu as pltpu
from jax.sharding import PartitionSpec as P

logit_scale = 10.0
log2_scale = logit_scale / math.log(2.0)

ROWS = 128
HALF = 64
CHUNKS = (32, 32)
PLANES = 8
MESH = pl.DeviceIdType.MESH

OFFSETS = (0, -1, -2, -3, 1, 2, 3, 4)
SLOT_OF = {o: i for i, o in enumerate(OFFSETS)}
SLOT_OF[-4] = 7


def scores_of(rows, cols):
    return log2_scale * lax.dot_general(
        rows, cols, (((1,), (1,)), ((), ())), preferred_element_type=jnp.float32
    )


def to_lanes(column):
    return jnp.transpose(jnp.broadcast_to(column, (ROWS, ROWS)))[0:1, :]


def to_sublanes(lanes):
    return jnp.transpose(jnp.broadcast_to(lanes, (ROWS, ROWS)))


def log_add(a, b):
    top = jnp.maximum(a, b)
    return top + jnp.log2(jnp.exp2(a - top) + jnp.exp2(b - top))


def kernel(
    both_ref, lab_ref, oimg_ref, otxt_ref, rimg_ref, rtxt_ref,
    cimg, ctxt, rimg, rtxt, scores, tscores, wide, gtxt, gsend,
    colp, sibrx, zmsg, zrx, drx, final, colx, rowp, rowrx, rsub, csub,
    ring_t, ring_i, sib_r, z_r, misc_s, misc_r, sent, loc_s,
):
    me = lax.axis_index("dp")
    z, x, k = me // 4, (me // 2) % 2, me % 2

    def device(plane, column, core):
        return {"dp": lax.rem(plane + PLANES, PLANES) * 4 + column * 2 + core}

    right, left = device(z + 1, x, k), device(z - 1, x, k)
    nbr, sib = device(z, 1 - x, k), device(z, x, 1 - k)
    held = (ctxt, cimg)
    rows_of = (rtxt, rimg)
    given = (both_ref.at[1], both_ref.at[0])

    def remote(src, dst, send, recv, to):
        return pltpu.make_async_remote_copy(
            src_ref=src, dst_ref=dst, send_sem=send, recv_sem=recv, device_id=to, device_id_type=MESH
        )

    def plane_of(slot):
        off = OFFSETS[slot] if isinstance(slot, int) else jnp.where(slot < 4, -slot, slot - 3)
        return lax.rem(z + off + PLANES, PLANES)

    def slot(d, s):
        return 0 if s == 0 else 7 if s == 4 else s + 3 * d

    def chunks(a, d, s):
        every = range(ROWS // CHUNKS[a])
        return [c for c in every if s < 4 or (c * CHUNKS[a] < HALF) == (d == 0)]

    def ring_id(a, d, s, c):
        before = [(e, t, b) for e in range(2) for t in range(1, 5) for b in chunks(a, e, t)]
        return before.index((d, s, c))

    def ring(a, d, s, c):
        part = pl.ds(c * CHUNKS[a], CHUNKS[a])
        src = given[a].at[part] if s == 1 else held[a].at[slot(d, s - 1), 0, part]
        arrived = (ring_t, ring_i)[a].at[ring_id(a, d, s, c)]
        return remote(src, held[a].at[slot(d, s), 0, part], sent.at[a], arrived, (right, left)[d])

    def to_sib(a, d, s):
        if s == 0:
            src, dst = given[a], held[a].at[0, 1]
        elif s == 4:
            part = pl.ds(HALF * d, HALF)
            src, dst = held[a].at[7, 0, part], held[a].at[7, 1, part]
        else:
            src, dst = held[a].at[slot(d, s), 0], held[a].at[slot(d, s), 1]
        return remote(src, dst, sent.at[2 + a], sib_r.at[a * 5 + s], sib)

    def misc(i, src, dst, to):
        return remote(src, dst, misc_s.at[i], misc_r.at[i], to)

    def rows_to_nbr(a):
        return misc(a, given[a], rows_of[a].at[0], nbr)

    def z_sums(p):
        there = SLOT_OF[-OFFSETS[p]] - 1
        return remote(zmsg, zrx.at[there], sent.at[4], z_r.at[0], device(z + OFFSETS[p], x, k))

    def z_rows(p):
        there = SLOT_OF[-OFFSETS[p]] - 1
        return remote(rowp.at[0], drx.at[there], sent.at[5], z_r.at[1], device(z + OFFSETS[p], 1 - x, k))

    def all_bytes(ref, sem):
        pltpu.make_async_copy(ref, ref, sem).wait()

    own = [
        pltpu.make_async_copy(given[0], ctxt.at[0, 0], loc_s.at[0]),
        pltpu.make_async_copy(given[1], rimg.at[1], loc_s.at[1]),
        pltpu.make_async_copy(given[1], cimg.at[0, 0], loc_s.at[2]),
        pltpu.make_async_copy(given[0], rtxt.at[1], loc_s.at[3]),
    ]
    barrier = pltpu.get_barrier_semaphore()
    peers = [right, left, nbr, sib]
    for p in peers:
        pl.semaphore_signal(barrier, inc=1, device_id=p, device_id_type=MESH)
    pl.semaphore_wait(barrier, len(peers))

    def first_sends(a):
        for c in chunks(a, 0, 1):
            for d in range(2):
                ring(a, d, 1, c).start()

    def step_thunks(a, s):
        def one(c):
            for d in range(2):
                if c in chunks(a, d, s):
                    ring(a, d, s, c).wait_recv()
                    if s < 4 and c in chunks(a, d, s + 1):
                        ring(a, d, s + 1, c).start()

        return [functools.partial(one, c) for c in chunks(a, 0, 1)]

    def ring_step(a, s, beside=()):
        beside = list(beside)
        for c in chunks(a, 0, 1):
            for d in range(2):
                if c in chunks(a, d, s):
                    ring(a, d, s, c).wait_recv()
                    if s < 4 and c in chunks(a, d, s + 1):
                        ring(a, d, s + 1, c).start()
            if beside:
                beside.pop(0)()
        for thunk in beside:
            thunk()
        for d in range(2):
            to_sib(a, d, s).start()

    def from_sib(a, s):
        if s == 4:
            all_bytes(held[a].at[7, 1], sib_r.at[a * 5 + 4])
        else:
            all_bytes(held[a].at[pl.ds(0, 2), 1], sib_r.at[a * 5 + s])

    first_sends(0)
    to_sib(0, 0, 0).start()
    rows_to_nbr(1).start()
    for c in own:
        c.start()

    row_peak = jnp.full((2 * ROWS, 1), -jnp.inf, jnp.float32)
    row_mass = jnp.zeros((2 * ROWS, 1), jnp.float32)

    def image_tile(q, peak, mass):
        s = scores_of(rimg[...].reshape(2 * ROWS, -1), ctxt[q].reshape(2 * ROWS, -1))
        scores[q] = s
        top = jnp.max(s, axis=0, keepdims=True)
        col = top + jnp.log2(jnp.sum(jnp.exp2(s - top), axis=0, keepdims=True))
        for kr in range(2):
            colp[kr, plane_of(q)] = col[:, kr * ROWS : (kr + 1) * ROWS]
        new_peak = jnp.maximum(peak, jnp.max(s, axis=1, keepdims=True))
        mass = mass * jnp.exp2(peak - new_peak) + jnp.sum(jnp.exp2(s - new_peak), axis=1, keepdims=True)
        return new_peak, mass

    def text_tile(q):
        tscores[q] = scores_of(rtxt[...].reshape(2 * ROWS, -1), cimg[q].reshape(2 * ROWS, -1))

    ring_step(0, 1)
    ring_step(0, 2)
    first_sends(1)
    own[0].wait()
    own[1].wait()
    rows_to_nbr(1).wait_recv()
    to_sib(0, 0, 0).wait_recv()
    row_peak, row_mass = image_tile(0, row_peak, row_mass)
    from_sib(0, 1)
    for q in (1, 4):
        row_peak, row_mass = image_tile(q, row_peak, row_mass)
    ring_step(0, 3)
    to_sib(1, 0, 0).start()
    rows_to_nbr(0).start()
    from_sib(0, 2)
    for q in (2, 5):
        row_peak, row_mass = image_tile(q, row_peak, row_mass)
    from_sib(0, 3)
    for q in (3, 6):
        row_peak, row_mass = image_tile(q, row_peak, row_mass)
    ring_step(0, 4, step_thunks(1, 1))
    for d in range(2):
        to_sib(1, d, 1).start()
    from_sib(0, 4)
    row_peak, row_mass = image_tile(7, row_peak, row_mass)

    col_to_sib = misc(2, colp.at[1], sibrx, sib)
    col_to_sib.start()
    row_part = row_peak + jnp.log2(row_mass)
    rowp[0] = to_lanes(row_part[:ROWS])
    rowp[1] = to_lanes(row_part[ROWS:])
    zmsg[8] = rowp[1]
    row_to_nbr = misc(3, rowp, rowrx, nbr)
    row_to_nbr.start()
    for p in range(1, 8):
        z_rows(p).start()
    col_to_sib.wait_recv()
    zmsg[:8] = log_add(colp[0], sibrx[...])
    for p in range(1, 8):
        z_sums(p).start()
    ring_step(1, 2)
    own[2].wait()
    own[3].wait()
    rows_to_nbr(0).wait_recv()
    to_sib(1, 0, 0).wait_recv()
    text_tile(0)
    row_to_nbr.wait_recv()
    row_nbr = log_add(rowp[0], rowrx[1])
    row_own = log_add(rowp[1], rowrx[0])
    final[0, 8 + z] = row_own
    rsub[:ROWS] = to_sublanes(row_nbr + 1.0)
    rsub[ROWS:] = to_sublanes(row_own + 1.0)
    from_sib(1, 1)
    text_tile(1)
    text_tile(4)
    ring_step(1, 3)
    from_sib(1, 2)
    text_tile(2)
    text_tile(5)
    all_bytes(zrx, z_r.at[0])
    all_bytes(drx, z_r.at[1])
    parts = [zmsg[:8]] + [zrx[p, :8] for p in range(7)]
    top = functools.reduce(jnp.maximum, parts)
    mass = sum(jnp.exp2(p - top) for p in parts)
    final[0, :8] = top + jnp.log2(mass)
    for p in range(1, 8):
        final[0, 8 + plane_of(p)] = log_add(zrx[p - 1, 8], drx[p - 1])
    final_to_sib = misc(4, final.at[0], final.at[1], sib)
    final_to_sib.start()
    col_to_nbr = misc(5, final.at[0, z], colx.at[0], nbr)
    col_to_nbr.start()
    final_to_sib.wait_recv()

    def lanes_of(side, q):
        plane = 8 * side + plane_of(q)
        return jnp.concatenate([final[0, plane], final[1, plane]], axis=1) + 1.0

    def weights_of(s, sub, lanes):
        return jnp.exp2(s - jnp.concatenate([sub, sub], axis=1)) + jnp.exp2(s - lanes)

    def products(half, count, tiles, sub, side, cols, positive=None):
        part = pl.ds(half * ROWS, ROWS)
        for q in range(count):
            w = weights_of(tiles[q, part], sub[part], lanes_of(side, q))
            if positive is not None and q == 0:
                mask = positive.astype(jnp.float32)
                w = w - jnp.concatenate([mask, jnp.zeros_like(mask)], axis=1)
            wide[part, q * 2 * ROWS : (q + 1) * 2 * ROWS] = w.astype(jnp.bfloat16)
        depth = count * 2 * ROWS
        return jnp.dot(
            wide[part, :depth], cols[:count].reshape(depth, -1), preferred_element_type=jnp.float32
        )

    gsend[0] = (logit_scale * products(0, 8, scores, rsub, 0, ctxt)).astype(jnp.bfloat16)
    gimg_to_nbr = misc(6, gsend.at[0], rimg_ref, nbr)
    gimg_to_nbr.start()

    for d in range(2):
        for c in chunks(1, d, 4):
            ring(1, d, 4, c).wait_recv()
        to_sib(1, d, 4).start()
    col_to_nbr.wait_recv()
    csub[:ROWS] = to_sublanes(colx[0] + 1.0)
    csub[ROWS:] = to_sublanes(final[0, z] + 1.0)
    from_sib(1, 3)
    text_tile(3)
    text_tile(6)

    gtxt[...] = products(0, 7, tscores, csub, 1, cimg)
    from_sib(1, 4)
    last = cimg[7].reshape(2 * ROWS, -1)
    w = weights_of(scores_of(rtxt[0], last), csub[:ROWS], lanes_of(1, 7)).astype(jnp.bfloat16)
    gsend[1] = (
        logit_scale * (gtxt[...] + jnp.dot(w, last, preferred_element_type=jnp.float32))
    ).astype(jnp.bfloat16)
    gtxt_to_nbr = misc(7, gsend.at[1], rtxt_ref, nbr)
    gtxt_to_nbr.start()

    labels = lab_ref[...] - me * ROWS
    label_rows = to_sublanes(labels.astype(jnp.float32))
    lane_ids = lax.broadcasted_iota(jnp.int32, (ROWS, ROWS), 1).astype(jnp.float32)
    row_ids = lax.broadcasted_iota(jnp.int32, (ROWS, ROWS), 0)
    text_tile(7)
    oimg_ref[...] = logit_scale * products(1, 8, scores, rsub, 0, ctxt, label_rows == lane_ids)
    otxt_ref[...] = logit_scale * products(1, 8, tscores, csub, 1, cimg, labels == row_ids)

    for a in range(2):
        all_bytes(held[a].at[pl.ds(0, 7), 0], sent.at[a])
        all_bytes(held[a].at[:, 0], sent.at[2 + a])
        rows_to_nbr(a).wait_send()
    all_bytes(zrx, sent.at[4])
    all_bytes(drx, sent.at[5])
    for c in (col_to_sib, row_to_nbr, final_to_sib, col_to_nbr, gimg_to_nbr, gtxt_to_nbr):
        c.wait_send()
    gimg_to_nbr.wait_recv()
    gtxt_to_nbr.wait_recv()


def local(image_emb, text_emb, labels):
    width = image_emb.shape[1]
    bf16, f32 = jnp.bfloat16, jnp.float32
    dma = pltpu.SemaphoreType.DMA
    block = jax.ShapeDtypeStruct((ROWS, width), f32)
    other = jax.ShapeDtypeStruct((ROWS, width), bf16)
    own_img, own_txt, nbr_img, nbr_txt = pl.pallas_call(
        kernel,
        out_shape=(block, block, other, other),
        in_specs=[
            pl.BlockSpec(memory_space=pl.ANY),
            pl.BlockSpec(memory_space=pltpu.VMEM),
        ],
        out_specs=(pl.BlockSpec(memory_space=pltpu.VMEM),) * 4,
        scratch_shapes=[
            pltpu.VMEM((PLANES, 2, ROWS, width), bf16),
            pltpu.VMEM((PLANES, 2, ROWS, width), bf16),
            pltpu.VMEM((2, ROWS, width), bf16),
            pltpu.VMEM((2, ROWS, width), bf16),
            pltpu.VMEM((PLANES, 2 * ROWS, 2 * ROWS), f32),
            pltpu.VMEM((PLANES, 2 * ROWS, 2 * ROWS), f32),
            pltpu.VMEM((2 * ROWS, PLANES * 2 * ROWS), bf16),
            pltpu.VMEM((ROWS, width), f32),
            pltpu.VMEM((2, ROWS, width), bf16),
            pltpu.VMEM((2, PLANES, 1, ROWS), f32),
            pltpu.VMEM((PLANES, 1, ROWS), f32),
            pltpu.VMEM((PLANES + 1, 1, ROWS), f32),
            pltpu.VMEM((PLANES - 1, PLANES + 1, 1, ROWS), f32),
            pltpu.VMEM((PLANES - 1, 1, ROWS), f32),
            pltpu.VMEM((2, 2 * PLANES, 1, ROWS), f32),
            pltpu.VMEM((1, 1, ROWS), f32),
            pltpu.VMEM((2, 1, ROWS), f32),
            pltpu.VMEM((2, 1, ROWS), f32),
            pltpu.VMEM((2 * ROWS, ROWS), f32),
            pltpu.VMEM((2 * ROWS, ROWS), f32),
            dma((7 * ROWS // CHUNKS[0],)),
            dma((7 * ROWS // CHUNKS[1],)),
            dma((10,)),
            dma((2,)),
            dma((8,)),
            dma((8,)),
            dma((6,)),
            dma((4,)),
        ],
        compiler_params=pltpu.CompilerParams(
            collective_id=0, has_side_effects=True, vmem_limit_bytes=32 * 1024 * 1024
        ),
        cost_estimate=pl.CostEstimate(
            flops=8 * 8 * 256 * 256 * 512, bytes_accessed=4 * 1024 * 1024, transcendentals=6 * 8 * 256 * 256
        ),
    )(jnp.stack([image_emb, text_emb]), labels.reshape(1, ROWS))
    return own_img + nbr_img.astype(f32), own_txt + nbr_txt.astype(f32)


def solution(mesh):
    rows = P(("rep", "dp"), None)
    return jax.shard_map(
        local,
        mesh=mesh,
        in_specs=(rows, rows, P(("rep", "dp"))),
        out_specs=(rows, rows),
        check_vma=False,
    )
```
